32 devices in a mesh: seq: 8 (over y, x, core), blk: 4 (over z).
Axes of the slice: x: 2, y: 2, z: 4, core: 2. Of those that a mesh axis runs over, the one named last changes fastest.
Arguments:
- stem_tokens: bfloat16 [128, 24, 128, 128], P('blk', 'seq'), may hold values from -6 to 6
- view_code: int32 [128, 24], P('blk', 'seq'), may hold values from 1 to 7
- cotangent: bfloat16 [2048, 24, 128], P('blk', 'seq'), may hold values from -6 to 6
- stem_queries: bfloat16 [16, 128], replicated, may hold values from -8 to 8
- w_stem_kv: bfloat16 [128, 256], replicated, may hold values from -0.5 to 0.5
- w_stem_out: bfloat16 [128, 128], replicated, may hold values from -1.5 to 1.5
- gain_one: float32 [128], replicated, may hold values from 0.1 to 1.9
- w_qkv: bfloat16 [128, 384], replicated, may hold values from -0.5 to 0.5
- w_attn_out: bfloat16 [128, 128], replicated, may hold values from -2 to 2
- gain_two: float32 [128], replicated, may hold values from 0.1 to 1.9
- w_up: bfloat16 [128, 512], replicated, may hold values from -0.5 to 0.5
- w_down: bfloat16 [512, 128], replicated, may hold values from -0.25 to 0.25
Outputs:
- block_out: bfloat16 [2048, 24, 128], P('blk', 'seq')
- grad_input: float32 [128, 24, 128, 128], P('blk', 'seq')
- grad_stem_queries: float32 [16, 128], P('blk')
- grad_w_stem_kv: float32 [128, 256], P('blk')
- grad_w_stem_out: float32 [128, 128], P('blk')
- grad_gain_one: float32 [128], P('blk')
- grad_w_qkv: float32 [128, 384], P('blk')
- grad_w_attn_out: float32 [128, 128], P('blk')
- grad_gain_two: float32 [128], P('blk')
- grad_w_up: float32 [128, 512], P('blk')
- grad_w_down: float32 [512, 128], P('blk')
The draws below stay inside these ranges and needn't reach their ends.
Inputs may be any that keep to these rules, and one draw needn't show every extreme that they name: `view_code`: bit v (v = 0, 1, 2) of a code is 1 where view v is present at that timestep; every timestep has a view.
All inputs are finite; a program needn't handle non-finite values.
Results may differ from the reference program's by a relative error of at most 0.02.
Values may be sent and summed in bfloat16 or wider, within the bound.
A program may use at most 128 MiB of HBM per device.

```python
import math
import jax
import jax.numpy as jnp
from jax import lax

D = 128
HEADS = 8
FF = 512
NQ = 16
IMG_TOK = 32
HD = 16
KEYS = 128
STEPS = 128
SEQS = 24
TOKENS = 2048


def set_ends(values, stream_key, smallest, largest):
    extent = values.shape
    index_at = [jax.random.randint(jax.random.fold_in(stream_key, axis), (), 0, extent[axis]) for axis in range(len(extent))]
    values = values.at[tuple(index_at)].set(smallest)
    longest = extent.index(max(extent))
    index_at[longest] = (index_at[longest] + 1) % extent[longest]
    return values.at[tuple(index_at)].set(largest)


def block_scale(stream_key, extent, cuts, least, top_value):
    level = 1.0
    for axis_at, shards_of in cuts:
        draws = jax.random.uniform(jax.random.fold_in(jax.random.fold_in(stream_key, 6), axis_at), (shards_of,), jnp.float32, least / len(cuts), top_value / len(cuts))
        level = level * jnp.repeat(jnp.exp(draws), extent[axis_at] // shards_of).reshape((-1,) + (1,) * (len(extent) - 1 - axis_at))
    return level


def bell_draw(stream_key, extent, spread, most, cuts=(), held_as=jnp.bfloat16):
    loudness = block_scale(stream_key, extent, cuts, -0.22, 0.18) if cuts else 1.0
    values = jax.random.normal(stream_key, extent, jnp.float32) * spread * loudness
    return jnp.minimum(jnp.maximum(values, -most), most).astype(held_as)


def setup_inputs(seed: int = 0) -> dict:
    splits = jax.random.split(jax.random.key(seed), 13)
    return {
        "stem_tokens": bell_draw(splits[0], (STEPS, SEQS, KEYS, D), 1.0, 6.0, ((0, 4), (1, 8))),
        "view_code": set_ends(jax.random.randint(splits[1], (STEPS, SEQS), 1, 8), jax.random.fold_in(splits[1], 1), 1, 7).astype(jnp.int32),
        "cotangent": bell_draw(splits[2], (TOKENS, SEQS, D), 1.0, 6.0, ((0, 4), (1, 8))),
        "stem_queries": bell_draw(splits[3], (NQ, D), 1.5, 8.0),
        "w_stem_kv": bell_draw(splits[4], (D, 2 * D), D ** -0.5, 0.5),
        "w_stem_out": bell_draw(splits[5], (D, D), (D // 8) ** -0.5, 1.5),
        "gain_one": jnp.clip(1.0 + 0.18 * jax.random.normal(splits[6], (D,), jnp.float32), 0.1, 1.9),
        "w_qkv": bell_draw(splits[7], (D, 3 * D), D ** -0.5, 0.5),
        "w_attn_out": bell_draw(splits[8], (D, D), (D // 16) ** -0.5, 2.0),
        "gain_two": jnp.clip(1.0 + 0.18 * jax.random.normal(splits[9], (D,), jnp.float32), 0.1, 1.9),
        "w_up": bell_draw(splits[10], (D, FF), D ** -0.5, 0.5),
        "w_down": bell_draw(splits[11], (FF, D), FF ** -0.5, 0.25),
    }


EPSILON = 1e-05
NEGATIVE_FILL = -1e+30
HIGHEST_PRECISION = lax.Precision.HIGHEST

@jax.custom_vjp
def low(v):
    return lax.optimization_barrier(v.astype(jnp.bfloat16)).astype(jnp.float32)

@jax.custom_vjp
def low_back(v):
    return v

def low_keep(v):
    return (low(v), None)

def low_pass(kept, grad):
    return (grad,)

def back_keep(v):
    return (v, None)

def back_low(kept, grad):
    return (low(grad),)
low.defvjp(low_keep, low_pass)
low_back.defvjp(back_keep, back_low)

def layer_norm(values_in, gain_vector):
    center = values_in - lax.optimization_barrier(jnp.mean(values_in, axis=-1, keepdims=True))
    variance = lax.optimization_barrier(jnp.mean(center * center, axis=-1, keepdims=True))
    return center * lax.rsqrt(variance + EPSILON) * gain_vector

def visible_keys(codes_seq):
    positions = jnp.arange(KEYS, dtype=jnp.int32)
    view_slot = jnp.minimum(positions // IMG_TOK, 2).astype(jnp.int32)
    present = jnp.right_shift(codes_seq[:, None].astype(jnp.int32), view_slot[None, :]) % 2
    return (present == 1) | (positions[None, :] >= 3 * IMG_TOK)

def stem_forward(tokens_seq, codes_seq, stem_queries, w_stem_kv, w_stem_out):
    score_scale = 1.0 / math.sqrt(HD)
    key_value = low(low_back(jnp.einsum('tkd,de->tke', tokens_seq, w_stem_kv, precision=HIGHEST_PRECISION)))
    stem_keys = key_value[:, :, :D].reshape(STEPS, KEYS, HEADS, HD)
    stem_values = key_value[:, :, D:].reshape(STEPS, KEYS, HEADS, HD)
    query_heads = stem_queries.reshape(NQ, HEADS, HD)
    scores = low_back(jnp.einsum('nhe,tkhe->thnk', query_heads, stem_keys, precision=HIGHEST_PRECISION) * score_scale)
    scores = jnp.where(visible_keys(codes_seq)[:, None, None, :], scores, NEGATIVE_FILL)
    attn_probs = jax.nn.softmax(scores, axis=-1)
    stem_mixed = low(low_back(jnp.einsum('thnk,tkhe->tnhe', low(attn_probs), stem_values, precision=HIGHEST_PRECISION)))
    stem_mixed = stem_mixed.reshape(STEPS, NQ, D)
    stem_output = low_back(jnp.einsum('tnd,de->tne', stem_mixed, w_stem_out, precision=HIGHEST_PRECISION))
    return stem_output.reshape(STEPS * NQ, D)

def trunk_attention(query_all, key_all, value_all):
    score_scale = 1.0 / math.sqrt(HD)
    seq_rows = query_all.shape[0]
    block_rows = min(512, seq_rows)
    block_count = seq_rows // block_rows
    key_steps = jnp.arange(seq_rows, dtype=jnp.int32) // NQ

    def one_block(operands):
        query_block, first_row = operands
        query_steps = (first_row + jnp.arange(block_rows, dtype=jnp.int32)) // NQ
        allowed = key_steps[None, :] <= query_steps[:, None]
        scores = low_back(jnp.einsum('rhe,che->hrc', query_block, key_all, precision=HIGHEST_PRECISION) * score_scale)
        scores = jnp.where(allowed[None], scores, NEGATIVE_FILL)
        attn_probs = jax.nn.softmax(scores, axis=-1)
        return low(low_back(jnp.einsum('hrc,che->rhe', low(attn_probs), value_all, precision=HIGHEST_PRECISION)))
    query_blocks = query_all.reshape(block_count, block_rows, HEADS, HD)
    first_rows = jnp.arange(block_count, dtype=jnp.int32) * block_rows
    attended = lax.map(jax.checkpoint(one_block), (query_blocks, first_rows))
    return attended.reshape(seq_rows, D)

def trunk_forward(residual, gain_one, w_qkv, w_attn_out, gain_two, w_up, w_down):
    seq_rows = residual.shape[0]
    normed_one = low(low_back(layer_norm(residual, gain_one)))
    projected = low(low_back(jnp.dot(normed_one, w_qkv, precision=HIGHEST_PRECISION)))
    query_all = projected[:, :D].reshape(seq_rows, HEADS, HD)
    key_all = projected[:, D:2 * D].reshape(seq_rows, HEADS, HD)
    value_all = projected[:, 2 * D:].reshape(seq_rows, HEADS, HD)
    attended = trunk_attention(query_all, key_all, value_all)
    after_attn = residual + low_back(jnp.dot(attended, w_attn_out, precision=HIGHEST_PRECISION))
    normed_two = low(low_back(layer_norm(after_attn, gain_two)))
    hidden_pre = low_back(jnp.dot(normed_two, w_up, precision=HIGHEST_PRECISION))
    hidden = low(jax.nn.gelu(hidden_pre, approximate=False))
    return after_attn + low_back(jnp.dot(hidden, w_down, precision=HIGHEST_PRECISION))

def reference(stem_tokens, view_code, cotangent, stem_queries, w_stem_kv, w_stem_out, gain_one, w_qkv, w_attn_out, gain_two, w_up, w_down):
    params_all = tuple((array.astype(jnp.float32) for array in (stem_queries, w_stem_kv, w_stem_out, gain_one, w_qkv, w_attn_out, gain_two, w_up, w_down)))

    def one_sequence(params_in, tokens_seq, codes_seq):
        residual = stem_forward(tokens_seq, codes_seq, params_in[0], params_in[1], params_in[2])
        return trunk_forward(residual, params_in[3], params_in[4], params_in[5], params_in[6], params_in[7], params_in[8])

    def scan_step(totals, operands):
        tokens_seq, codes_seq, grad_seq = operands

        def forward_only(params_in, tokens_in):
            return one_sequence(params_in, tokens_in, codes_seq)
        block_full, pullback = jax.vjp(forward_only, params_all, tokens_seq.astype(jnp.float32))
        grad_params, grad_tokens = pullback(grad_seq.astype(jnp.float32))
        totals = jax.tree.map(jnp.add, totals, grad_params)
        return (totals, (block_full.astype(jnp.bfloat16), grad_tokens))
    zero_totals = jax.tree.map(jnp.zeros_like, params_all)
    scanned = (jnp.transpose(stem_tokens, (1, 0, 2, 3)), jnp.transpose(view_code, (1, 0)), jnp.transpose(cotangent, (1, 0, 2)))
    totals, stacked = lax.scan(scan_step, zero_totals, scanned)
    block_out = jnp.transpose(stacked[0], (1, 0, 2))
    grad_input = jnp.transpose(stacked[1], (1, 0, 2, 3))
    return (block_out, grad_input, totals[0], totals[1], totals[2], totals[3], totals[4], totals[5], totals[6], totals[7], totals[8])
```

```python
import functools
import math

import jax
import jax.numpy as jnp
from jax import lax
from jax.experimental import pallas as pl
from jax.experimental.pallas import tpu as pltpu
from jax.sharding import PartitionSpec as P

HEADS = 8
HEAD = 16
VIEWS = 3
GROUP = 8
EPSILON = 1e-05
FILL = -1e30
LOG2E = math.log2(math.e)
BF = jnp.bfloat16
F32 = jnp.float32
VMEM_BYTES = 58 * 2**20


def dot(left, right):
    return jnp.dot(left, right, preferred_element_type=F32)


def dot_nt(left, right):
    return lax.dot_general(left, right, (((1,), (1,)), ((), ())), preferred_element_type=F32)


def dot_tn(left, right):
    return lax.dot_general(left, right, (((0,), (0,)), ((), ())), preferred_element_type=F32)


def column_norm(values):
    center = values - jnp.mean(values, axis=0, keepdims=True)
    inverse = lax.rsqrt(jnp.mean(center * center, axis=0, keepdims=True) + EPSILON)
    return center * inverse, inverse


def column_norm_back(grad_unit, unit, inverse):
    centered = grad_unit - jnp.mean(grad_unit, axis=0, keepdims=True)
    return inverse * (centered - unit * jnp.mean(grad_unit * unit, axis=0, keepdims=True))


def stem_forward(s, x_ref, bias_ref, w1, block_mask, gather, wso_t, wqkv_t, gain, v_ref, p_ref, mix_ref, res_ref, n1_ref, send):
    steps, seqs = x_ref.shape[0], x_ref.shape[1]
    keys = x_ref.shape[2]
    view = keys // (VIEWS + 1)

    def group_body(g, carry):
        parts = []
        for k in range(GROUP):
            t = g * GROUP + k
            both = dot(x_ref[t, s], w1[...])
            values = both[:, :128].astype(BF)
            v_ref[s, t] = values
            rows = [
                both[view * i : view * (i + 1), 128:] + bias_ref[(i * steps + t) * seqs + s]
                for i in range(VIEWS)
            ]
            scores = jnp.concatenate(rows + [both[view * VIEWS :, 128:]], axis=0)
            top = jnp.max(scores, axis=0, keepdims=True)
            weights = jnp.exp2(scores - top)
            total = jnp.sum(weights, axis=0, keepdims=True)
            probs = (weights * (1.0 / total)).astype(BF)
            p_ref[s, t] = probs
            parts.append((dot_tn(values, probs) * block_mask[...]).astype(BF))
        mixed = dot(jnp.concatenate(parts, axis=1), gather[...])
        mix_ref[s, :, pl.ds(pl.multiple_of(g * 128, 128), 128)] = mixed.astype(BF)
        return carry

    lax.fori_loop(0, steps // GROUP, group_body, 0)
    residual = dot(wso_t[...], mix_ref[s])
    res_ref[s] = residual
    unit, _ = column_norm(residual)
    normed = (unit * gain[...]).astype(BF)
    n1_ref[s] = normed
    projected = dot(wqkv_t[...], normed)
    rows = projected.shape[0] // send.shape[0]
    per = rows // 3
    for j in range(send.shape[0]):
        part = projected[j * rows : (j + 1) * rows]
        send[j, s, 0:per, :] = (part[:per] * (LOG2E / math.sqrt(HEAD))).astype(BF)
        send[j, s, per:, :] = part[per:].astype(BF)


def attend_forward(s, att, onehot, mask_rows, ka_ref, o_ref, ob_ref, l_ref):
    tokens = att.shape[2]
    block = ob_ref.shape[3]
    zeros16 = jnp.zeros((16, block), BF)
    zeros32 = jnp.zeros((32, block), BF)
    stacked = jnp.concatenate(
        [att[s, 32:64, :], onehot[...], jnp.zeros((64, tokens), BF)], axis=0
    )
    ka_ref[...] = stacked.T

    def first(a, i):
        query = att[s, 16 * a : 16 * a + 16, block * i : block * (i + 1)]
        query = [query, zeros16] if a == 0 else [zeros16, query]
        tail = jnp.zeros((64, block), BF)
        scores = []
        if i:
            plain = jnp.concatenate(query + [zeros32, tail], axis=0)
            scores.append(dot(ka_ref[0 : block * i, :], plain))
        masked = jnp.concatenate(query + [mask_rows[...], tail], axis=0)
        scores.append(dot(ka_ref[block * i : block * (i + 1), :], masked))
        top = functools.reduce(jnp.maximum, [jnp.max(x, axis=0, keepdims=True) for x in scores])
        return scores, top

    def second(a, i, scores, top):
        start, out, total = 0, 0.0, 0.0
        for piece in scores:
            for c in range(0, piece.shape[0], block):
                weights = jnp.exp2(piece[c : c + block] - top)
                total = total + jnp.sum(weights, axis=0, keepdims=True)
                values = att[s, 64 + 16 * a : 80 + 16 * a, start : start + block]
                out = out + dot(values, weights.astype(BF))
                start += block
        out = out * (1.0 / total)
        o_ref[s, 16 * a : 16 * a + 16, block * i : block * (i + 1)] = out
        ob_ref[i, s, 16 * a : 16 * a + 16, :] = out.astype(BF)
        l_ref[s, a : a + 1, block * i : block * (i + 1)] = top + jnp.log2(total)

    units = [(a, i) for i in range(tokens // block) for a in range(2)]
    held = None
    for unit in units:
        now = first(*unit)
        if held is not None:
            second(*held[0], *held[1])
        held = (unit, now)
    second(*held[0], *held[1])


def feed_forward(s, orecv, res_ref, cot_ref, w, gain_row, out_ref, ga_ref, send, g_up, g_down, g_ao, g_gain):
    attended = jnp.concatenate([orecv[j, s] for j in range(orecv.shape[0])], axis=0)
    after = res_ref[s] + dot(w["ao_t"][...], attended)
    unit, inverse = column_norm(after)
    normed = (unit * gain_row[...]).astype(BF)
    pre = dot(w["up_t"][...], normed)
    cdf = 0.5 + 0.5 * lax.erf(pre * (1.0 / math.sqrt(2.0)))
    hidden = (pre * cdf).astype(BF)
    slope = cdf + pre * (jnp.exp2(pre * pre * (-0.5 * LOG2E)) * (1.0 / math.sqrt(2.0 * math.pi)))
    out_ref[s] = (after + dot(w["down_t"][...], hidden)).astype(BF)
    cot = cot_ref[s]
    g_down[...] += dot_nt(hidden, cot)
    grad_pre = (dot(w["down"][...], cot) * slope).astype(BF)
    g_up[...] += dot_nt(normed, grad_pre)
    grad_normed = dot(w["up"][...], grad_pre)
    g_gain[...] += grad_normed * unit
    grad_after = cot.astype(F32) + column_norm_back(grad_normed * gain_row[...], unit, inverse)
    ga_ref[s] = grad_after
    low = grad_after.astype(BF)
    g_ao[...] += dot_nt(attended, low)
    grad_att = dot(w["ao"][...], low).astype(BF)
    rows = grad_att.shape[0] // send.shape[0]
    for j in range(send.shape[0]):
        send[j, s] = grad_att[j * rows : (j + 1) * rows]


def three_parts(row):
    first = row.astype(BF).astype(F32)
    second = (row - first).astype(BF).astype(F32)
    return [first, second, row - first - second]


def attend_backward(s, att, dob, o_ref, l_ref, onehot, qa_ref, kb_ref, kd_ref, vb_ref, dq_ref, dk_ref, dv_ref, send):
    tokens = att.shape[2]
    block = send.shape[3]
    count = tokens // block
    rows = []
    dots = []
    for a in range(2):
        head = slice(16 * a, 16 * a + 16)
        rows += three_parts(-l_ref[s, a : a + 1, :])
        product = dob[s, head, :].astype(F32) * o_ref[s, head, :]
        down = -jnp.sum(product, axis=0, keepdims=True)
        high = down.astype(BF).astype(F32)
        dots += [high, down - high]
    small = jnp.concatenate(rows + dots + [jnp.zeros((6, tokens), F32)], axis=0).astype(BF)
    stacked = jnp.concatenate(
        [att[s, 0:32, :], dob[s], small, onehot[...], jnp.zeros((16, tokens), BF)], axis=0
    )
    qa_ref[...] = stacked.T
    for a in range(2):
        keys = att[s, 32 + 16 * a : 48 + 16 * a, :]
        kb_ref[a, 16 * a : 16 * a + 16, :] = keys
        kd_ref[a, 16 * a : 16 * a + 16, :] = keys
        vb_ref[a, 32 + 16 * a : 48 + 16 * a, :] = att[s, 64 + 16 * a : 80 + 16 * a, :]

    def span(i):
        return slice(block * i, block * (i + 1))

    def first(a, i, j):
        left = qa_ref[span(i), :]
        keys = kd_ref if i == j else kb_ref
        return dot(left, keys[a, :, span(j)]), dot(left, vb_ref[a, :, span(j)])

    def second(a, i, j, scores, grads):
        probs = jnp.exp2(scores)
        low = probs.astype(BF)
        grad = (probs * grads).astype(BF)
        head = slice(16 * a, 16 * a + 16)
        add_v = dot(dob[s, head, span(i)], low)
        add_k = dot(att[s, head, span(i)], grad)
        add_q = dot_nt(att[s, 32 + 16 * a : 48 + 16 * a, span(j)], grad)
        if i == j:
            dv_ref[head, span(j)] = add_v
            dk_ref[head, span(j)] = add_k
        else:
            dv_ref[head, span(j)] += add_v
            dk_ref[head, span(j)] += add_k
        if j == 0:
            dq_ref[head, span(i)] = add_q
        else:
            dq_ref[head, span(i)] += add_q

    units = [(a, i, j) for j in range(count) for i in range(j, count) for a in range(2)]
    held = None
    for unit in units:
        now = first(*unit)
        if held is not None:
            second(*held[0], *held[1])
        held = (unit, now)
    second(*held[0], *held[1])
    for i in range(count):
        send[i, s, 0:32, :] = (dq_ref[:, span(i)] * 0.25).astype(BF)
        send[i, s, 32:64, :] = (dk_ref[:, span(i)] * math.log(2.0)).astype(BF)
        send[i, s, 64:96, :] = dv_ref[:, span(i)].astype(BF)


def attend_constants(ones_ref, mask_ref, kb_ref, kd_ref, vb_ref):
    kb_ref[...] = jnp.zeros_like(kb_ref)
    kd_ref[...] = jnp.zeros_like(kd_ref)
    vb_ref[...] = jnp.zeros_like(vb_ref)
    for a in range(2):
        kb_ref[a, 64:80, :] = ones_ref[a]
        kd_ref[a, 64:80, :] = ones_ref[a]
        kd_ref[a, 80:112, :] = mask_ref[...]
        vb_ref[a, 64:80, :] = ones_ref[2 + a]


def stem_backward(s, x_ref, v_ref, p_ref, mix_ref, res_ref, n1_ref, ga_ref, precv, block_mask, spread, w, gain, gin_ref, gm_ref, g_qkv, g_gain, g_so, g_kv):
    steps = x_ref.shape[0]
    grad_proj = jnp.concatenate([precv[j, s] for j in range(precv.shape[0])], axis=0)
    g_qkv[...] += dot_nt(n1_ref[s], grad_proj)
    grad_normed = dot(w["qkv"][...], grad_proj)
    unit, inverse = column_norm(res_ref[s])
    g_gain[...] += grad_normed * unit
    grad_res = ga_ref[s] + column_norm_back(grad_normed * gain[...], unit, inverse)
    low = grad_res.astype(BF)
    g_so[...] += dot_nt(mix_ref[s], low)
    gm_ref[...] = dot(w["so"][...], low).astype(BF)

    def group_body(g, carry):
        wide = dot(gm_ref[:, pl.ds(pl.multiple_of(g * 128, 128), 128)], spread[...])
        total = jnp.zeros((128, 256), F32)
        for k in range(GROUP):
            t = g * GROUP + k
            grad_mixed = (wide[:, 128 * k : 128 * (k + 1)] * block_mask[...]).astype(BF)
            probs = p_ref[s, t]
            grad_probs = dot(v_ref[s, t], grad_mixed)
            weighted = probs.astype(F32) * grad_probs
            down = jnp.sum(weighted, axis=0, keepdims=True)
            grad_scores = (weighted - probs.astype(F32) * down).astype(BF)
            grad_values = dot_nt(probs, grad_mixed).astype(BF)
            both = jnp.concatenate([grad_values, grad_scores], axis=1)
            gin_ref[t, s] = dot(both, w["in"][...])
            total = total + dot_tn(x_ref[t, s], both)
        g_kv[...] += total
        return carry

    lax.fori_loop(0, steps // GROUP, group_body, 0)


def params():
    return pltpu.CompilerParams(vmem_limit_bytes=VMEM_BYTES)


def shape(dims, dtype):
    return jax.ShapeDtypeStruct(dims, dtype)


def per_device(
    stem_tokens, view_code, cotangent, stem_queries, w_stem_kv, w_stem_out,
    gain_one, w_qkv, w_attn_out, gain_two, w_up, w_down, nblk,
):
    steps, seqs, keys, width = stem_tokens.shape
    queries = stem_queries.shape[0]
    own = steps * queries
    tokens = own * nblk
    ff = w_up.shape[1]
    scale = 1.0 / math.sqrt(HEAD)
    lane = jnp.arange(128)
    block_mask = (lane[:, None] // HEAD == lane[None, :] // queries).astype(F32)
    row = jnp.arange(GROUP * 128)
    gather = ((row[:, None] // 128 == lane[None, :] // queries) & (row[:, None] % queries == lane[None, :] % queries)).astype(BF)
    spread = gather.T
    position = jnp.arange(tokens)
    onehot = ((position[None, :] // queries) % 32 == jnp.arange(32)[:, None]).astype(BF)
    local = jnp.arange(512) // queries
    mask_rows = jnp.where(jnp.arange(32)[:, None] > local[None, :], FILL, 0.0).astype(BF)
    mask_cols = jnp.where((position[None, :] // queries) % 32 > jnp.arange(32)[:, None], FILL, 0.0).astype(BF)
    patterns = [[0, 1, 2], [3, 4, 5], [6, 7], [8, 9]]
    ones_rows = jnp.stack([jnp.broadcast_to(sum((jnp.arange(16) == r) for r in rows)[:, None], (16, tokens)) for rows in patterns]).astype(BF)
    query_blocks = jnp.where(lane[:, None] // queries == lane[None, :] // HEAD, jnp.tile(stem_queries.astype(F32), (HEADS, 1)), 0.0)
    w_keys = w_stem_kv[:, :width].astype(F32)
    fold = jnp.dot(w_keys, query_blocks.T, precision=lax.Precision.HIGHEST) * scale
    w1 = jnp.concatenate([w_stem_kv[:, width:], (fold * LOG2E).astype(BF)], axis=1)
    w_in = jnp.concatenate([w_stem_kv[:, width:].T, fold.T.astype(BF)], axis=0)
    per = HEADS // nblk * HEAD
    order = w_qkv.reshape(width, 3, nblk, per).transpose(0, 2, 1, 3)
    wqkv = order.reshape(width, 3 * width)
    wqkv_t = wqkv.T
    present = jnp.stack([(view_code >> i) % 2 for i in range(VIEWS)])
    bias = jnp.where(present == 1, 0.0, FILL).astype(F32).reshape(-1)
    cot = cotangent.transpose(1, 2, 0)
    g1, g2 = gain_one[:, None], gain_two[:, None]
    vm = pl.BlockSpec(memory_space=pltpu.VMEM)
    sm = pl.BlockSpec(memory_space=pltpu.SMEM)

    def k_stem(x, b, w1_, bm, ga, so, qk, g, v, p, mix, res, n1, send):
        for s in range(seqs):
            stem_forward(s, x, b, w1_, bm, ga, so, qk, g, v, p, mix, res, n1, send)

    v_all, p_all, mix, res, n1, qkv_send = pl.pallas_call(
        k_stem,
        out_shape=[
            shape((seqs, steps, keys, 128), BF), shape((seqs, steps, keys, 128), BF), shape((seqs, 128, own), BF),
            shape((seqs, 128, own), F32), shape((seqs, 128, own), BF), shape((nblk, seqs, 3 * per, own), BF),
        ],
        in_specs=[vm, sm] + [vm] * 6, out_specs=[vm] * 6, compiler_params=params(),
    )(stem_tokens, bias, w1, block_mask, gather, w_stem_out.T, wqkv_t, g1)
    qkv = lax.all_to_all(qkv_send, "blk", 0, 0, tiled=True)
    att = qkv.transpose(1, 2, 0, 3).reshape(seqs, 3 * per, tokens)

    def k_att(att_, oh, mr, o, ob, l, ka):
        for s in range(seqs):
            attend_forward(s, att_, oh, mr, ka, o, ob, l)

    o_all, o_send, l_all = pl.pallas_call(
        k_att,
        out_shape=[shape((seqs, per, tokens), F32), shape((nblk, seqs, per, own), BF), shape((seqs, 8, tokens), F32)],
        in_specs=[vm] * 3, out_specs=[vm] * 3,
        scratch_shapes=[pltpu.VMEM((tokens, 128), BF)], compiler_params=params(),
    )(att, onehot, mask_rows)
    o_recv = lax.all_to_all(o_send, "blk", 0, 0, tiled=True)

    def k_ffn(orecv, res_, cot_, ao_t, up_t, down_t, ao, up, down, g, out, ga, send, g_up, g_down, g_ao, g_gain):
        w = {"ao_t": ao_t, "up_t": up_t, "down_t": down_t, "ao": ao, "up": up, "down": down}
        for ref in (g_up, g_down, g_ao, g_gain):
            ref[...] = jnp.zeros_like(ref)
        for s in range(seqs):
            feed_forward(s, orecv, res_, cot_, w, g, out, ga, send, g_up, g_down, g_ao, g_gain)

    out, ga, do_send, g_up, g_down, g_ao, g_gain2 = pl.pallas_call(
        k_ffn,
        out_shape=[
            shape((seqs, 128, own), BF), shape((seqs, 128, own), F32), shape((nblk, seqs, per, own), BF),
            shape((128, ff), F32), shape((ff, 128), F32), shape((128, 128), F32), shape((128, own), F32),
        ],
        in_specs=[vm] * 10, out_specs=[vm] * 7, compiler_params=params(),
    )(o_recv, res, cot, w_attn_out.T, w_up.T, w_down.T, w_attn_out, w_up, w_down, g2)
    do = lax.all_to_all(do_send, "blk", 0, 0, tiled=True).transpose(1, 2, 0, 3).reshape(seqs, per, tokens)

    def k_back(att_, do_, o, l, oh, on, mc, send, qa, kb, kd, vb, dq, dk, dv):
        attend_constants(on, mc, kb, kd, vb)
        for s in range(seqs):
            attend_backward(s, att_, do_, o, l, oh, qa, kb, kd, vb, dq, dk, dv, send)

    dp_send = pl.pallas_call(
        k_back,
        out_shape=shape((nblk, seqs, 3 * per, own), BF),
        in_specs=[vm] * 7, out_specs=vm,
        scratch_shapes=[pltpu.VMEM((tokens, 128), BF)] + [pltpu.VMEM((2, 128, tokens), BF)] * 3 + [pltpu.VMEM((per, tokens), F32)] * 3,
        compiler_params=params(),
    )(att, do, o_all, l_all, onehot, ones_rows, mask_cols)
    dp_recv = lax.all_to_all(dp_send, "blk", 0, 0, tiled=True)

    def k_stemb(x, v, p, mx, rs, n, ga_, pr, bm, sp, wq, wso, win, g, gin, g_qkv, g_gain, g_so, g_kv, gm):
        w = {"qkv": wq, "so": wso, "in": win}
        for ref in (g_qkv, g_gain, g_so, g_kv):
            ref[...] = jnp.zeros_like(ref)
        for s in range(seqs):
            stem_backward(s, x, v, p, mx, rs, n, ga_, pr, bm, sp, w, g, gin, gm, g_qkv, g_gain, g_so, g_kv)

    gin, g_qkv, g_gain1, g_so, g_kv = pl.pallas_call(
        k_stemb,
        out_shape=[
            shape((steps, seqs, keys, 128), F32), shape((128, 3 * width), F32), shape((128, own), F32),
            shape((128, 128), F32), shape((128, 256), F32),
        ],
        in_specs=[vm] * 14, out_specs=[vm] * 5,
        scratch_shapes=[pltpu.VMEM((128, own), BF)], compiler_params=params(),
    )(stem_tokens, v_all, p_all, mix, res, n1, ga, dp_recv, block_mask, spread, wqkv, w_stem_out, w_in, g1)

    g_value, g_fold = g_kv[:, :128], g_kv[:, 128:] * scale
    g_keys = jnp.dot(g_fold, query_blocks, precision=lax.Precision.HIGHEST)
    cross = jnp.dot(g_fold.T, w_keys, precision=lax.Precision.HIGHEST).reshape(HEADS, queries, HEADS, HEAD)
    g_queries = jnp.einsum("hnhe->nhe", cross).reshape(queries, width)
    g_qkv = g_qkv.reshape(width, nblk, 3, per).transpose(0, 2, 1, 3).reshape(width, 3 * width)
    grads = [
        g_queries, jnp.concatenate([g_keys, g_value], axis=1), g_so, jnp.sum(g_gain1, axis=1),
        g_qkv, g_ao, jnp.sum(g_gain2, axis=1), g_up, g_down,
    ]
    sizes = [g.size // nblk for g in grads]
    flat = jnp.concatenate([g.reshape(nblk, -1) for g in grads], axis=1)
    flat = lax.psum(flat, "seq")
    mine = lax.psum_scatter(flat, "blk", scatter_dimension=0, tiled=True).reshape(-1)
    results, at = [], 0
    for g, size in zip(grads, sizes):
        results.append(mine[at : at + size].reshape((g.shape[0] // nblk,) + g.shape[1:]))
        at += size
    return (out.transpose(2, 0, 1), gin, *results)


def solution(mesh):
    return jax.shard_map(
        functools.partial(per_device, nblk=mesh.shape["blk"]),
        mesh=mesh,
        in_specs=(P("blk", "seq"), P("blk", "seq"), P("blk", "seq")) + (P(),) * 9,
        out_specs=(P("blk", "seq"), P("blk", "seq")) + (P("blk"),) * 9,
        check_vma=False,
    )
```

```python
import functools
import math

import jax
import jax.numpy as jnp
import ml_dtypes
import numpy as np
from jax import lax
from jax.experimental import pallas as pl
from jax.experimental.pallas import tpu as pltpu
from jax.sharding import PartitionSpec as P

HEADS = 8
HEAD = 16
VIEWS = 3
GROUP = 8
EPSILON = 1e-05
FILL = -1e30
LOG2E = math.log2(math.e)
BF = jnp.bfloat16
F32 = jnp.float32
VMEM_BYTES = 58 * 2**20


def dot(left, right):
    return jnp.dot(left, right, preferred_element_type=F32)


def dot_nt(left, right):
    return lax.dot_general(left, right, (((1,), (1,)), ((), ())), preferred_element_type=F32)


def dot_tn(left, right):
    return lax.dot_general(left, right, (((0,), (0,)), ((), ())), preferred_element_type=F32)


def column_norm(values):
    center = values - jnp.mean(values, axis=0, keepdims=True)
    inverse = lax.rsqrt(jnp.mean(center * center, axis=0, keepdims=True) + EPSILON)
    return center * inverse, inverse


def column_norm_back(grad_unit, unit, inverse):
    centered = grad_unit - jnp.mean(grad_unit, axis=0, keepdims=True)
    return inverse * (centered - unit * jnp.mean(grad_unit * unit, axis=0, keepdims=True))


def stem_forward(s, r):
    steps, keys = r.x.shape[1], r.x.shape[2]
    view = keys // (VIEWS + 1)

    def group_body(g, carry):
        first = g * GROUP
        both = dot(r.x[s, pl.ds(first, GROUP)].reshape(GROUP * keys, 128), r.w1[...])
        values = both[:, :128].astype(BF)
        r.v[s, pl.ds(first, GROUP)] = values.reshape(GROUP, keys, 128)
        scores = []
        for k in range(GROUP):
            code = r.code[first + k, s]
            for i in range(VIEWS + 1):
                at = keys * k + view * i
                rows = both[at : at + view, 128:]
                if i < VIEWS:
                    rows = rows + (((code >> i) & 1) - 1).astype(F32) * (-FILL)
                scores.append(rows)
        scores = jnp.concatenate(scores, axis=0).reshape(GROUP, keys, 128)
        top = jnp.max(scores, axis=1, keepdims=True)
        weights = jnp.exp2(scores - top)
        inverse = 1.0 / jnp.sum(weights, axis=1, keepdims=True)
        probs = weights.astype(BF)
        r.p[s, pl.ds(first, GROUP)] = probs
        r.rl[s, pl.ds(first, GROUP)] = inverse
        mixed = [dot_tn(values[keys * k : keys * (k + 1)], probs[k]) for k in range(GROUP)]
        mixed = [(mixed[k] * (r.block_mask[...] * inverse[k])).astype(BF) for k in range(GROUP)]
        gathered = dot(jnp.concatenate(mixed, axis=1), r.gather[...])
        r.mix[s, :, pl.ds(pl.multiple_of(g * 128, 128), 128)] = gathered.astype(BF)
        return carry

    lax.fori_loop(0, steps // GROUP, group_body, 0)
    residual = dot(r.wso_t[...], r.mix[s])
    r.res[s] = residual
    unit, _ = column_norm(residual)
    normed = (unit * r.gain1[...]).astype(BF)
    r.n1[s] = normed
    projected = dot(r.wqkv_t[...], normed)
    send = r.qkv_send
    rows = projected.shape[0] // send.shape[0]
    per = rows // 3
    for j in range(send.shape[0]):
        part = projected[j * rows : (j + 1) * rows]
        send[j, s, 0:per, :] = (part[:per] * (LOG2E / math.sqrt(HEAD))).astype(BF)
        send[j, s, per:, :] = part[per:].astype(BF)


def attend_forward(s, r):
    att, onehot, mask_rows, ka_ref, o_ref, ob_ref, l_ref = r.att, r.onehot, r.mask_rows, r.ka, r.o, r.o_send, r.l
    tokens = att.shape[2]
    block = ob_ref.shape[3]
    zeros16 = jnp.zeros((16, block), BF)
    zeros32 = jnp.zeros((32, block), BF)
    stacked = jnp.concatenate(
        [att[s, 32:64, :], onehot[...], jnp.zeros((64, tokens), BF)], axis=0
    )
    ka_ref[...] = stacked.T

    def first(a, i):
        query = att[s, 16 * a : 16 * a + 16, block * i : block * (i + 1)]
        query = [query, zeros16] if a == 0 else [zeros16, query]
        tail = jnp.zeros((64, block), BF)
        scores = []
        if i:
            plain = jnp.concatenate(query + [zeros32, tail], axis=0)
            scores.append(dot(ka_ref[0 : block * i, :], plain))
        masked = jnp.concatenate(query + [mask_rows[...], tail], axis=0)
        scores.append(dot(ka_ref[block * i : block * (i + 1), :], masked))
        top = functools.reduce(jnp.maximum, [jnp.max(x, axis=0, keepdims=True) for x in scores])
        return scores, top

    def second(a, i, scores, top):
        start, out, total = 0, 0.0, 0.0
        for piece in scores:
            for c in range(0, piece.shape[0], block):
                weights = jnp.exp2(piece[c : c + block] - top)
                total = total + jnp.sum(weights, axis=0, keepdims=True)
                values = att[s, 64 + 16 * a : 80 + 16 * a, start : start + block]
                out = out + dot(values, weights.astype(BF))
                start += block
        out = out * (1.0 / total)
        o_ref[s, 16 * a : 16 * a + 16, block * i : block * (i + 1)] = out
        ob_ref[i, s, 16 * a : 16 * a + 16, :] = out.astype(BF)
        l_ref[s, a : a + 1, block * i : block * (i + 1)] = top + jnp.log2(total)

    units = [(a, i) for i in range(tokens // block) for a in range(2)]
    held = None
    for unit in units:
        now = first(*unit)
        if held is not None:
            second(*held[0], *held[1])
        held = (unit, now)
    second(*held[0], *held[1])


def feed_forward(s, r):
    orecv, send = r.o_recv, r.do_send
    attended = jnp.concatenate([orecv[j, s] for j in range(orecv.shape[0])], axis=0)
    after = r.res[s] + dot(r.wao_t[...], attended)
    unit, inverse = column_norm(after)
    normed = (unit * r.gain2[...]).astype(BF)
    pre = dot(r.wup_t[...], normed)
    cdf = 0.5 + 0.5 * lax.erf(pre * (1.0 / math.sqrt(2.0)))
    hidden = (pre * cdf).astype(BF)
    slope = cdf + pre * (jnp.exp2(pre * pre * (-0.5 * LOG2E)) * (1.0 / math.sqrt(2.0 * math.pi)))
    r.out[s] = (after + dot(r.wdown_t[...], hidden)).astype(BF)
    cot = r.cot[s]
    r.g_down[...] += dot_nt(hidden, cot)
    grad_pre = (dot(r.wdown[...], cot) * slope).astype(BF)
    r.g_up[...] += dot_nt(normed, grad_pre)
    grad_normed = dot(r.wup[...], grad_pre)
    r.g_gain2[...] += grad_normed * unit
    grad_after = cot.astype(F32) + column_norm_back(grad_normed * r.gain2[...], unit, inverse)
    r.ga[s] = grad_after
    low = grad_after.astype(BF)
    r.g_ao[...] += dot_nt(attended, low)
    grad_att = dot(r.wao[...], low).astype(BF)
    rows = grad_att.shape[0] // send.shape[0]
    for j in range(send.shape[0]):
        send[j, s] = grad_att[j * rows : (j + 1) * rows]


def three_parts(row):
    first = row.astype(BF).astype(F32)
    second = (row - first).astype(BF).astype(F32)
    return [first, second, row - first - second]


def attend_backward(s, r):
    att, dob, o_ref, l_ref, onehot, send = r.att, r.dob, r.o, r.l, r.onehot, r.p_send
    qa_ref, kb_ref, kd_ref, vb_ref, dq_ref, dk_ref, dv_ref = r.qa, r.kb, r.kd, r.vb, r.dq, r.dk, r.dv
    tokens = att.shape[2]
    block = send.shape[3]
    count = tokens // block
    rows = []
    dots = []
    for a in range(2):
        head = slice(16 * a, 16 * a + 16)
        rows += three_parts(-l_ref[s, a : a + 1, :])
        product = dob[s, head, :].astype(F32) * o_ref[s, head, :]
        down = -jnp.sum(product, axis=0, keepdims=True)
        high = down.astype(BF).astype(F32)
        dots += [high, down - high]
    small = jnp.concatenate(rows + dots + [jnp.zeros((6, tokens), F32)], axis=0).astype(BF)
    stacked = jnp.concatenate(
        [att[s, 0:32, :], dob[s], small, onehot[...], jnp.zeros((16, tokens), BF)], axis=0
    )
    qa_ref[...] = stacked.T
    for a in range(2):
        keys = att[s, 32 + 16 * a : 48 + 16 * a, :]
        kb_ref[a, 16 * a : 16 * a + 16, :] = keys
        kd_ref[a, 16 * a : 16 * a + 16, :] = keys
        vb_ref[a, 32 + 16 * a : 48 + 16 * a, :] = att[s, 64 + 16 * a : 80 + 16 * a, :]

    def span(i):
        return slice(block * i, block * (i + 1))

    def first(a, i, j):
        left = qa_ref[span(i), :]
        keys = kd_ref if i == j else kb_ref
        return dot(left, keys[a, :, span(j)]), dot(left, vb_ref[a, :, span(j)])

    def second(a, i, j, scores, grads):
        probs = jnp.exp2(scores)
        low = probs.astype(BF)
        grad = (probs * grads).astype(BF)
        head = slice(16 * a, 16 * a + 16)
        add_v = dot(dob[s, head, span(i)], low)
        add_k = dot(att[s, head, span(i)], grad)
        add_q = dot_nt(att[s, 32 + 16 * a : 48 + 16 * a, span(j)], grad)
        if i == j:
            dv_ref[head, span(j)] = add_v
            dk_ref[head, span(j)] = add_k
        else:
            dv_ref[head, span(j)] += add_v
            dk_ref[head, span(j)] += add_k
        if j == 0:
            dq_ref[head, span(i)] = add_q
        else:
            dq_ref[head, span(i)] += add_q

    units = [(a, i, j) for j in range(count) for i in range(j, count) for a in range(2)]
    held = None
    for unit in units:
        now = first(*unit)
        if held is not None:
            second(*held[0], *held[1])
        held = (unit, now)
    second(*held[0], *held[1])
    for i in range(count):
        send[i, s, 0:32, :] = (dq_ref[:, span(i)] * 0.25).astype(BF)
        send[i, s, 32:64, :] = (dk_ref[:, span(i)] * math.log(2.0)).astype(BF)
        send[i, s, 64:96, :] = dv_ref[:, span(i)].astype(BF)


def attend_constants(r):
    for ref in (r.kb, r.kd, r.vb):
        ref[...] = jnp.zeros_like(ref)
    for a in range(2):
        r.kb[a, 64:80, :] = r.ones_rows[a]
        r.kd[a, 64:80, :] = r.ones_rows[a]
        r.kd[a, 80:112, :] = r.mask_cols[...]
        r.vb[a, 64:80, :] = r.ones_rows[2 + a]


def projection_backward(s, r):
    grad_proj = jnp.concatenate([r.p_recv[j, s] for j in range(r.p_recv.shape[0])], axis=0)
    r.g_qkv[...] += dot_nt(grad_proj, r.n1[s])
    grad_normed = dot(r.wqkv[...], grad_proj)
    unit, inverse = column_norm(r.res[s])
    r.g_gain1[...] += grad_normed * unit
    grad_res = r.ga[s] + column_norm_back(grad_normed * r.gain1[...], unit, inverse)
    low = grad_res.astype(BF)
    r.g_so[...] += dot_nt(r.mix[s], low)
    r.gm[s] = dot(r.wso[...], low).astype(BF)


def stem_backward(s, r):
    steps, keys = r.x.shape[1], r.x.shape[2]

    def group_body(g, carry):
        first = g * GROUP
        wide = dot(r.gm[s, :, pl.ds(pl.multiple_of(g * 128, 128), 128)], r.spread[...])
        inverse = r.rl[s, pl.ds(first, GROUP)]
        grad_mixed = [
            (wide[:, 128 * k : 128 * (k + 1)] * (r.block_mask[...] * inverse[k])).astype(BF)
            for k in range(GROUP)
        ]
        probs = r.p[s, pl.ds(first, GROUP)]
        values = r.v[s, pl.ds(first, GROUP)]
        grad_probs = [dot(values[k], grad_mixed[k]) for k in range(GROUP)]
        grad_values = [dot_nt(probs[k], grad_mixed[k]).astype(BF) for k in range(GROUP)]
        both = []
        for k in range(GROUP):
            weights = probs[k].astype(F32)
            down = jnp.sum(weights * grad_probs[k], axis=0, keepdims=True) * inverse[k]
            grad_scores = (weights * (grad_probs[k] - down)).astype(BF)
            both.append(jnp.concatenate([grad_values[k], grad_scores], axis=1))
        both = jnp.concatenate(both, axis=0)
        r.gin[s, pl.ds(first, GROUP)] = dot(both, r.w_in[...]).astype(BF).reshape(GROUP, keys, 128)
        r.g_kv[...] += dot_tn(r.x[s, pl.ds(first, GROUP)].reshape(GROUP * keys, 128), both)
        return carry

    lax.fori_loop(0, steps // GROUP, group_body, 0)


def prepare(r):
    queries = r.stem_queries.shape[0]
    tiled = jnp.concatenate([r.stem_queries[...]] * HEADS, axis=0)
    blocks = (tiled.astype(F32) * r.block_mask[...]).astype(BF)
    r.q_blocks[...] = blocks
    scale = 1.0 / math.sqrt(HEAD)
    w_keys, w_values = r.w_stem_kv[:, :128], r.w_stem_kv[:, 128:]
    r.w1[:, :128] = w_values
    r.w1[:, 128:] = (dot_nt(w_keys, blocks) * (scale * LOG2E)).astype(BF)
    r.w_in[:128] = w_values.T
    r.w_in[128:] = (dot_nt(blocks, w_keys) * scale).astype(BF)
    r.wso_t[...] = r.wso[...].T
    turned = r.w_qkv[...].T
    nblk = r.qkv_send.shape[0]
    per = 128 // nblk
    for j in range(nblk):
        for i in range(3):
            at = (3 * j + i) * per
            r.wqkv_t[at : at + per] = turned[128 * i + per * j : 128 * i + per * (j + 1)]
    r.wqkv[...] = r.wqkv_t[...].T
    r.wao_t[...] = r.wao[...].T
    r.wup_t[...] = r.wup[...].T
    r.wdown_t[...] = r.wdown[...].T
    own = r.gain1.shape[1]
    r.gain1[...] = jnp.broadcast_to(r.gain_one[...], (own, 128)).T
    r.gain2[...] = jnp.broadcast_to(r.gain_two[...], (own, 128)).T
    for ref in (r.g_qkv, r.g_gain1, r.g_so, r.g_kv, r.g_up, r.g_down, r.g_ao, r.g_gain2):
        ref[...] = jnp.zeros_like(ref)


def lane_sums(values):
    width = values.shape[0]
    folded = sum(values[:, width * i : width * (i + 1)] for i in range(values.shape[1] // width))
    return jnp.sum(folded.T, axis=0, keepdims=True)


def pack_ffn(r):
    nblk = r.pack0.shape[0]
    up, down, out = r.g_up[...].astype(BF), r.g_down[...].astype(BF), r.g_ao[...].astype(BF)
    rows = 128 // nblk
    wide, tall = up.shape[1] // 128, down.shape[0] // nblk
    for b in range(nblk):
        for i in range(wide):
            r.pack0[b, rows * i : rows * (i + 1)] = up[rows * b : rows * (b + 1), 128 * i : 128 * (i + 1)]
        at = rows * wide
        r.pack0[b, at : at + tall] = down[tall * b : tall * (b + 1)]
        r.pack0[b, at + tall : at + tall + rows] = out[rows * b : rows * (b + 1)]
        spare = r.pack0.shape[1] - (at + tall + rows)
        if spare:
            r.pack0[b, at + tall + rows :] = jnp.zeros((spare, 128), BF)


def pack_projection(r):
    nblk = r.pack1.shape[0]
    per = rows = 128 // nblk
    for i in range(3):
        natural = [r.g_qkv[(3 * j + i) * per : (3 * j + i + 1) * per] for j in range(nblk)]
        turned = jnp.concatenate(natural, axis=0).T.astype(BF)
        for b in range(nblk):
            r.pack1[b, rows * i : rows * (i + 1)] = turned[rows * b : rows * (b + 1)]
    out = r.g_so[...].astype(BF)
    for b in range(nblk):
        r.pack1[b, 3 * rows : 4 * rows] = out[rows * b : rows * (b + 1)]
        spare = r.pack1.shape[1] - 4 * rows
        if spare:
            r.pack1[b, 4 * rows :] = jnp.zeros((spare, 128), BF)


def pack_stem(r):
    nblk = r.pack2.shape[0]
    rows = 128 // nblk
    scale = 1.0 / math.sqrt(HEAD)
    fold = r.g_kv[:, 128:] * scale
    high = fold.astype(BF)
    keys = dot(high, r.q_blocks[...]) + dot((fold - high.astype(F32)).astype(BF), r.q_blocks[...])
    w_keys = r.w_stem_kv[:, :128]
    fold_t = fold.T
    high_t = fold_t.astype(BF)
    cross = dot(high_t, w_keys) + dot((fold_t - high_t.astype(F32)).astype(BF), w_keys)
    queries = r.stem_queries.shape[0]
    cross = cross * r.block_mask[...]
    summed = sum(cross[queries * h : queries * (h + 1)] for h in range(HEADS))
    keys, values = keys.astype(BF), r.g_kv[:, :128].astype(BF)
    gains = [lane_sums(r.g_gain1[...]), lane_sums(r.g_gain2[...])]
    gains = jnp.concatenate(gains + [jnp.zeros((14, 128), F32)], axis=0).astype(BF)
    for b in range(nblk):
        r.pack2[b, 0:rows] = keys[rows * b : rows * (b + 1)]
        r.pack2[b, rows : 2 * rows] = values[rows * b : rows * (b + 1)]
        r.pack2[b, 2 * rows : 2 * rows + 16] = summed.astype(BF)
        r.pack2[b, 2 * rows + 16 : 2 * rows + 32] = gains
        spare = r.pack2.shape[1] - (2 * rows + 32)
        if spare:
            r.pack2[b, 2 * rows + 32 :] = jnp.zeros((spare, 128), BF)


class Reduce:
    def __init__(self, r, index, pack, near, part, far, full):
        self.r, self.index = r, index
        self.pack, self.near, self.part, self.far, self.full = pack, near, part, far, full
        self.nseq, self.nblk = near.shape[0], far.shape[0]
        self.rows = full.shape[1]

    def copy(self, phase, k):
        r = self.r
        if phase == 1:
            peer, axis = lax.rem(r.my_blk + k, self.nblk), "blk"
            source, target = self.part.at[peer], self.far.at[r.my_blk]
        else:
            peer, axis = lax.rem(r.my_seq + k, self.nseq), "seq"
            if phase == 0:
                at = pl.multiple_of(peer * self.rows, self.rows)
                source, target = self.pack.at[:, pl.ds(at, self.rows)], self.near.at[r.my_seq]
            else:
                source, target = self.full.at[r.my_seq], self.full.at[r.my_seq]
        return pltpu.make_async_remote_copy(
            src_ref=source, dst_ref=target,
            send_sem=r.red_send.at[self.index, phase, k], recv_sem=r.red_recv.at[self.index, phase, k],
            device_id={axis: peer}, device_id_type=pl.DeviceIdType.MESH,
        )

    def each(self, phase, act):
        def body(k, carry):
            act(self.copy(phase, k))
            return carry

        lax.fori_loop(1, self.nblk if phase == 1 else self.nseq, body, 0)

    def start(self, phase):
        r = self.r
        if phase == 0:
            at = pl.multiple_of(r.my_seq * self.rows, self.rows)
            self.near[r.my_seq] = self.pack[:, pl.ds(at, self.rows)]
        if phase == 1:
            def add(i, total):
                return total + self.near[i].astype(F32)

            total = lax.fori_loop(1, self.nseq, add, self.near[0].astype(F32))
            self.part[...] = total.astype(BF)
            self.far[r.my_blk] = self.part[r.my_blk]
        if phase == 2:
            total = self.far[0].astype(F32)
            for b in range(1, self.nblk):
                total = total + self.far[b].astype(F32)
            self.full[r.my_seq] = total.astype(BF)
        self.each(phase, lambda c: c.start())

    def arrive(self, phase):
        self.each(phase, lambda c: c.wait_recv())

    def sent(self):
        for phase in range(3):
            self.each(phase, lambda c: c.wait_send())


def exchange(r, kind, s, k):
    nblk = r.qkv_send.shape[0]
    own = r.o_send.shape[3]
    peer = lax.rem(r.my_blk + k, nblk)
    lanes = pl.ds(pl.multiple_of(r.my_blk * own, own), own)
    source, target = {
        0: lambda: (r.qkv_send.at[peer, s], r.att.at[s, :, lanes]),
        1: lambda: (r.o_send.at[peer, s], r.o_recv.at[r.my_blk, s]),
        2: lambda: (r.do_send.at[peer, s], r.dob.at[s, :, lanes]),
        3: lambda: (r.p_send.at[peer, s], r.p_recv.at[r.my_blk, s]),
    }[kind]()
    return pltpu.make_async_remote_copy(
        src_ref=source, dst_ref=target,
        send_sem=r.ex_send.at[kind, s, k], recv_sem=r.ex_recv.at[kind, s, k],
        device_id={"blk": peer}, device_id_type=pl.DeviceIdType.MESH,
    )


def exchange_start(r, kind, s):
    nblk = r.qkv_send.shape[0]
    own = r.o_send.shape[3]
    for k in range(1, nblk):
        exchange(r, kind, s, k).start()
    lanes = pl.ds(pl.multiple_of(r.my_blk * own, own), own)
    if kind == 0:
        r.att[s, :, lanes] = r.qkv_send[r.my_blk, s]
    elif kind == 1:
        r.o_recv[r.my_blk, s] = r.o_send[r.my_blk, s]
    elif kind == 2:
        r.dob[s, :, lanes] = r.do_send[r.my_blk, s]
    else:
        r.p_recv[r.my_blk, s] = r.p_send[r.my_blk, s]


def exchange_arrive(r, kind, s):
    for k in range(1, r.qkv_send.shape[0]):
        exchange(r, kind, s, k).wait_recv()


class Refs:
    pass


def trunk_kernel(names, nseq, nblk, *refs):
    r = Refs()
    for name, ref in zip(names, refs, strict=True):
        setattr(r, name, ref)
    seqs = r.x.shape[0]
    r.my_seq, r.my_blk = lax.axis_index("seq"), lax.axis_index("blk")
    barrier = pltpu.get_barrier_semaphore()
    for axis, me, count in (("seq", r.my_seq, nseq), ("blk", r.my_blk, nblk)):
        def greet(k, carry, axis=axis, me=me, count=count):
            pl.semaphore_signal(
                barrier, inc=1, device_id={axis: lax.rem(me + k, count)}, device_id_type=pl.DeviceIdType.MESH
            )
            return carry

        lax.fori_loop(1, count, greet, 0)

    def load(s):
        return pltpu.make_async_copy(r.x_hbm.at[:, s], r.x.at[s], r.load_sem.at[0, s])

    def store(s):
        return pltpu.make_async_copy(r.gin.at[s], r.gin_hbm.at[:, s], r.load_sem.at[1, s])

    for s in range(seqs):
        load(s).start()
    prepare(r)
    reduces = [
        Reduce(r, i, getattr(r, f"pack{i}"), getattr(r, f"near{i}"), getattr(r, f"part{i}"), getattr(r, f"far{i}"), getattr(r, f"full{i}"))
        for i in range(3)
    ]
    for s in range(seqs):
        load(s).wait()
        stem_forward(s, r)
        if s == 0:
            pl.semaphore_wait(barrier, nseq + nblk - 2)
        exchange_start(r, 0, s)
    attend_constants(r)

    def stage_b(s):
        exchange_arrive(r, 0, s)
        attend_forward(s, r)
        exchange_start(r, 1, s)

    def stage_c(s):
        exchange_arrive(r, 1, s)
        feed_forward(s, r)
        exchange_start(r, 2, s)

    def stage_d(s):
        exchange_arrive(r, 2, s)
        attend_backward(s, r)
        exchange_start(r, 3, s)

    def stage_e(s):
        exchange_arrive(r, 3, s)
        projection_backward(s, r)

    order = []
    last = seqs - 1
    for s in range(seqs + 2):
        if s < seqs:
            order.append((stage_b, s))
        if 0 <= s - 1 < seqs:
            order.append((stage_c, s - 1))
        if 0 <= s - 2 < seqs:
            order.append((stage_d, s - 2))
    for stage, s in order:
        if (stage, s) == (stage_d, last):
            pass
        stage(s)
        if (stage, s) == (stage_c, last):
            pack_ffn(r)
            reduces[0].start(0)
    for s in range(seqs):
        stage_e(s)
        if s == 0:
            reduces[0].arrive(0)
            reduces[0].start(1)
        if s == last:
            pack_projection(r)
            reduces[1].start(0)
        stem_backward(s, r)
        store(s).start()
        if s == 0:
            reduces[0].arrive(1)
            reduces[0].start(2)
    pack_stem(r)
    reduces[2].start(0)
    reduces[1].arrive(0)
    reduces[1].start(1)
    reduces[2].arrive(0)
    reduces[2].start(1)
    reduces[1].arrive(1)
    reduces[1].start(2)
    reduces[2].arrive(1)
    reduces[2].start(2)
    for i in range(3):
        reduces[i].arrive(2)
        reduces[i].sent()
    for s in range(seqs):
        store(s).wait()
        for kind in range(4):
            for k in range(1, nblk):
                exchange(r, kind, s, k).wait_send()


def finish_kernel(nblk, gin, full0, full1, full2, o_gin, o_q, o_kv, o_so, o_g1, o_qkv, o_ao, o_g2, o_up, o_down):
    o_gin[...] = gin[...].astype(F32)
    rows = 128 // nblk
    me = lax.axis_index("blk")

    @pl.when(pl.program_id(0) == 0)
    def _():
        first = full0[...].astype(F32)
        wide, tall = o_up.shape[1] // 128, o_down.shape[0]
        for i in range(wide):
            o_up[:, 128 * i : 128 * (i + 1)] = first[rows * i : rows * (i + 1)]
        at = rows * wide
        o_down[...] = first[at : at + tall]
        o_ao[...] = first[at + tall : at + tall + rows]
        second = full1[...].astype(F32)
        for i in range(3):
            o_qkv[:, 128 * i : 128 * (i + 1)] = second[rows * i : rows * (i + 1)]
        o_so[...] = second[3 * rows : 4 * rows]
        third = full2[...].astype(F32)
        o_kv[:, :128] = third[0:rows]
        o_kv[:, 128:] = third[rows : 2 * rows]
        queries, part = third[2 * rows : 2 * rows + 16], o_q.shape[0]
        gains = third[2 * rows + 16 : 2 * rows + 32]
        o_q[...] = sum(jnp.where(me == b, queries[part * b : part * (b + 1)], 0.0) for b in range(nblk))
        mine = sum(jnp.where(me == b, gains[:, rows * b : rows * (b + 1)], 0.0) for b in range(nblk))
        o_g1[...] = mine[0:1]
        o_g2[...] = mine[1:2]


def shape(dims, dtype):
    return jax.ShapeDtypeStruct(dims, dtype)


def constants(steps_own, nblk, queries):
    lane = np.arange(128)
    tokens = steps_own * queries * nblk
    block_mask = lane[:, None] // HEAD == lane[None, :] // queries
    row = np.arange(GROUP * 128)
    gather = (row[:, None] // 128 == lane[None, :] // queries) & (row[:, None] % queries == lane[None, :] % queries)
    step = np.arange(tokens) // queries % steps_own
    slot = np.arange(steps_own)
    onehot = step[None, :] == slot[:, None]
    local = np.arange(steps_own * queries) // queries
    mask_rows = np.where(slot[:, None] > local[None, :], FILL, 0.0)
    mask_cols = np.where(step[None, :] > slot[:, None], FILL, 0.0)
    ones_rows = np.zeros((4, 16, tokens))
    for i, rows in enumerate(((0, 1, 2), (3, 4, 5), (6, 7), (8, 9))):
        ones_rows[i, list(rows)] = 1.0
    low = [jnp.asarray(c.astype(ml_dtypes.bfloat16)) for c in (gather, gather.T, onehot, mask_rows, mask_cols, ones_rows)]
    return [jnp.asarray(block_mask.astype(np.float32)), *low]


def per_device(
    stem_tokens, view_code, cotangent, stem_queries, w_stem_kv, w_stem_out,
    gain_one, w_qkv, w_attn_out, gain_two, w_up, w_down, nseq, nblk,
):
    steps, seqs, keys, width = stem_tokens.shape
    queries = stem_queries.shape[0]
    own = steps * queries
    tokens = own * nblk
    ff = w_up.shape[1]
    per = width // nblk
    vm = pl.BlockSpec(memory_space=pltpu.VMEM)
    sm = pl.BlockSpec(memory_space=pltpu.SMEM)
    anywhere = pl.BlockSpec(memory_space=pl.ANY)

    def pad(rows):
        return -(-rows // (16 * nseq)) * 16

    slices = [pad(per * ff // 128 + ff // nblk + per), pad(4 * per), pad(2 * per + 32)]
    inputs = {
        "x_hbm": (stem_tokens, anywhere), "code": (view_code, sm), "cot": (cotangent.transpose(1, 2, 0), vm),
        "stem_queries": (stem_queries, vm), "w_stem_kv": (w_stem_kv, vm), "wso": (w_stem_out, vm),
        "gain_one": (gain_one.reshape(1, width), vm), "w_qkv": (w_qkv, vm), "wao": (w_attn_out, vm),
        "gain_two": (gain_two.reshape(1, width), vm), "wup": (w_up, vm), "wdown": (w_down, vm),
    }
    names = ("block_mask", "gather", "spread", "onehot", "mask_rows", "mask_cols", "ones_rows")
    for name, value in zip(names, constants(steps, nblk, queries), strict=True):
        inputs[name] = (value, vm)
    outputs = {
        "out": (shape((seqs, width, own), BF), vm),
        "gin_hbm": (shape((steps, seqs, keys, width), BF), anywhere),
        "full0": (shape((nseq, slices[0], 128), BF), vm),
        "full1": (shape((nseq, slices[1], 128), BF), vm),
        "full2": (shape((nseq, slices[2], 128), BF), vm),
    }
    scratch = {
        "x": ((seqs, steps, keys, width), BF), "v": ((seqs, steps, keys, width), BF), "p": ((seqs, steps, keys, width), BF),
        "gin": ((seqs, steps, keys, width), BF), "rl": ((seqs, steps, 1, 128), F32),
        "mix": ((seqs, 128, own), BF), "res": ((seqs, 128, own), F32), "n1": ((seqs, 128, own), BF),
        "ga": ((seqs, 128, own), F32), "gm": ((seqs, 128, own), BF),
        "qkv_send": ((nblk, seqs, 3 * per, own), BF), "att": ((seqs, 3 * per, tokens), BF),
        "o_send": ((nblk, seqs, per, own), BF), "o_recv": ((nblk, seqs, per, own), BF),
        "do_send": ((nblk, seqs, per, own), BF), "dob": ((seqs, per, tokens), BF),
        "p_send": ((nblk, seqs, 3 * per, own), BF), "p_recv": ((nblk, seqs, 3 * per, own), BF),
        "o": ((seqs, per, tokens), F32), "l": ((seqs, 8, tokens), F32),
        "ka": ((tokens, 128), BF), "qa": ((tokens, 128), BF),
        "kb": ((2, 128, tokens), BF), "kd": ((2, 128, tokens), BF), "vb": ((2, 128, tokens), BF),
        "dq": ((per, tokens), F32), "dk": ((per, tokens), F32), "dv": ((per, tokens), F32),
        "w1": ((128, 256), BF), "w_in": ((256, 128), BF), "q_blocks": ((128, 128), BF), "wso_t": ((128, 128), BF),
        "wqkv_t": ((384, 128), BF), "wqkv": ((128, 384), BF), "wao_t": ((128, 128), BF),
        "wup_t": ((ff, 128), BF), "wdown_t": ((128, ff), BF), "gain1": ((128, own), F32), "gain2": ((128, own), F32),
        "g_qkv": ((384, 128), F32), "g_gain1": ((128, own), F32), "g_so": ((128, 128), F32), "g_kv": ((128, 256), F32),
        "g_up": ((128, ff), F32), "g_down": ((ff, 128), F32), "g_ao": ((128, 128), F32), "g_gain2": ((128, own), F32),
    }
    for i, rows in enumerate(slices):
        scratch[f"pack{i}"] = ((nblk, nseq * rows, 128), BF)
        scratch[f"near{i}"] = ((nseq, nblk, rows, 128), BF)
        scratch[f"part{i}"] = ((nblk, rows, 128), BF)
        scratch[f"far{i}"] = ((nblk, rows, 128), BF)
    semaphores = {
        "ex_send": (4, seqs, nblk), "ex_recv": (4, seqs, nblk),
        "red_send": (3, 3, max(nseq, nblk)), "red_recv": (3, 3, max(nseq, nblk)), "load_sem": (2, seqs),
    }
    names = [*inputs, *outputs, *scratch, *semaphores]
    out, gin, *full = pl.pallas_call(
        functools.partial(trunk_kernel, names, nseq, nblk),
        out_shape=[o[0] for o in outputs.values()],
        in_specs=[i[1] for i in inputs.values()],
        out_specs=[o[1] for o in outputs.values()],
        scratch_shapes=[pltpu.VMEM(*v) for v in scratch.values()] + [pltpu.SemaphoreType.DMA(v) for v in semaphores.values()],
        compiler_params=pltpu.CompilerParams(
            vmem_limit_bytes=VMEM_BYTES, collective_id=0, has_side_effects=True
        ),
    )(*[i[0] for i in inputs.values()])
    full = [f.reshape(-1, 128) for f in full]

    def whole(*dims):
        return pl.BlockSpec(dims, lambda t: (0,) * len(dims))

    chunk = 4
    big = pl.BlockSpec((chunk, seqs, keys, width), lambda t: (t, 0, 0, 0))
    dims = [(queries // nblk, width), (per, 2 * width), (per, width), (1, per), (per, 3 * width), (per, width), (1, per), (per, ff), (ff // nblk, width)]
    gin, *grads = pl.pallas_call(
        functools.partial(finish_kernel, nblk),
        grid=(steps // chunk,),
        out_shape=[shape((steps, seqs, keys, width), F32)] + [shape(d, F32) for d in dims],
        in_specs=[big] + [whole(*f.shape) for f in full],
        out_specs=[big] + [whole(*d) for d in dims],
        compiler_params=pltpu.CompilerParams(vmem_limit_bytes=VMEM_BYTES),
    )(gin, *full)
    for i in (3, 6):
        grads[i] = grads[i].reshape(-1)
    return (out.transpose(2, 0, 1), gin, *grads)


def solution(mesh):
    return jax.shard_map(
        functools.partial(per_device, nseq=mesh.shape["seq"], nblk=mesh.shape["blk"]),
        mesh=mesh,
        in_specs=(P("blk", "seq"), P("blk", "seq"), P("blk", "seq")) + (P(),) * 9,
        out_specs=(P("blk", "seq"), P("blk", "seq")) + (P("blk"),) * 9,
        check_vma=False,
    )
```
